32 devices in a mesh: shard: 4 (over z), ctx: 4 (over y, x), tp: 2 (over core).
Axes of the slice: x: 2, y: 2, z: 4, core: 2. Of those that a mesh axis runs over, the one named last changes fastest.
Arguments:
- layer_entry_input: bfloat16 [2048, 1024], P(('shard', 'ctx')), may hold values from -6 to 6
- first_layer_values: bfloat16 [2048, 1024], P(('shard', 'ctx'), 'tp'), may hold values from -6 to 6
- segments: int32 [2048], P(('shard', 'ctx')), may hold values from 0 to 2, as said below
- cotangent: bfloat16 [2048, 1024], P(('shard', 'ctx')), may hold values from -6 to 6
- layernorm_gain: bfloat16 [2, 1024], P(None, 'shard'), may hold values from 0.5 to 1.5
- layernorm_bias: bfloat16 [2, 1024], P(None, 'shard'), may hold values from -1.75 to 1.75
- token_shift_coefs: bfloat16 [7, 1024], P(None, 'shard'), may hold values from 0 to 1
- channel_coefficients: bfloat16 [8, 16, 64], P(None, 'tp', 'shard'), may hold values from -10 to 4
- receptance_key_value_weight: bfloat16 [3, 1024, 1024], P(None, 'shard', 'tp'), may hold values from -0.1875 to 0.1875
- output_weight: bfloat16 [1024, 1024], P('tp', 'shard'), may hold values from -0.375 to 0.375
- low_rank_down: bfloat16 [1024, 288], P('shard'), may hold values from -0.1875 to 0.1875
- low_rank_upper: bfloat16 [288, 1024], P('shard', 'tp'), may hold values from -0.75 to 0.75
- channel_key_weight: bfloat16 [1024, 4096], P('shard', 'tp'), may hold values from -0.1875 to 0.1875
- channel_value_weight: bfloat16 [4096, 1024], P('tp', 'shard'), may hold values from -0.09375 to 0.09375
Outputs:
- layer_output: bfloat16 [2048, 1024], P(('shard', 'ctx'))
- grad_x: float32 [2048, 1024], P(('shard', 'ctx'))
- grad_value_first: float32 [2048, 1024], P(('shard', 'ctx'), 'tp')
- grad_norm_gain: float32 [2, 1024], P(None, 'shard')
- grad_norm_bias: float32 [2, 1024], P(None, 'shard')
- grad_mix_coef: float32 [6, 1024], P(None, 'shard')
- grad_decay_mix: float32 [1024], P('shard')
- grad_head_coef: float32 [8, 16, 64], P(None, 'tp', 'shard')
- grad_w_rkv: float32 [3, 1024, 1024], P(None, 'shard', 'tp')
- grad_w_out: float32 [1024, 1024], P('tp', 'shard')
- grad_lora_down: float32 [1024, 288], P('shard')
- grad_lora_up: float32 [288, 1024], P('shard', 'tp')
- grad_w_ffn_in: float32 [1024, 4096], P('shard', 'tp')
- grad_w_ffn_out: float32 [4096, 1024], P('tp', 'shard')
The draws below stay inside these ranges and needn't reach their ends.
Inputs may be any that keep to these rules, and one draw needn't show every extreme that they name: `segments`: each sequence holds exactly three documents numbered 0, 1, 2 in order; document 1 starts within the first 128 tokens of the sequence and ends within its last 128 tokens.
All inputs are finite; a program needn't handle non-finite values.
Results may differ from the reference program's by a relative error of at most 0.025.
The reference program's roundings to bfloat16 on the way count: a program that leaves them out, or rounds other values in their place, can miss the bound.
Values may be sent and summed in bfloat16 or wider, within the bound.
A program may use at most 128 MiB of HBM per device.

```python
import math
import jax
import jax.numpy as jnp
from jax import lax

H = 16
HS = 64
MODEL_WIDTH = 1024
FF = 4096
DECAY_LOW_RANK = 64
RATE_RANK = 64
VALUE_RANK = 32
LOW_RANK_TOTAL = 288
BLK = 128
SEQS = 4
SEQ_LEN = 512
TOKENS = 2048


def draw_segments(key, part):
    key = jax.random.fold_in(key, 11)
    first_key, last_key = jax.random.split(key)
    starts = jax.random.randint(first_key, (SEQS, 1), 1, BLK)
    ends = jax.random.randint(last_key, (SEQS, 1), SEQ_LEN - BLK + 1, SEQ_LEN)
    position = jnp.arange(SEQ_LEN)[None, :]
    numbers = (position >= starts).astype(jnp.int32) + (position >= ends).astype(jnp.int32)
    return numbers.reshape(TOKENS)


def draw_channel_coefficients(key, part):
    key = jax.random.fold_in(key, 7)
    lookup_vectors = jax.random.split(key, 9)
    dimension_sizes = (H, HS)
    level = jax.random.uniform(lookup_vectors[0], (H, 1), minval=-8.0, maxval=-1.0)
    fading_baseline = jnp.clip(level + 0.5 * jax.random.normal(lookup_vectors[1], dimension_sizes), -10.0, 0.0)
    learning_speed_baseline = jax.random.uniform(lookup_vectors[2], dimension_sizes, minval=-5.0, maxval=-1.0)
    content_baseline = jnp.clip(jax.random.normal(lookup_vectors[3], dimension_sizes), -4.0, 4.0)
    lookup_unit_multiplier = jax.random.uniform(lookup_vectors[4], dimension_sizes, minval=0.5, maxval=1.5)
    lookup_speed_multiplier = jax.random.uniform(lookup_vectors[5], dimension_sizes, minval=0.0, maxval=1.0)
    current_step_extra = jnp.clip(0.5 * jax.random.normal(lookup_vectors[6], dimension_sizes), -2.0, 2.0)
    cluster_normalize_multiplier = jax.random.uniform(lookup_vectors[7], dimension_sizes, minval=0.5, maxval=1.5)
    cluster_normalize_shift = jnp.clip(0.5 * jax.random.normal(lookup_vectors[8], dimension_sizes), -2.0, 2.0)
    return jnp.stack([fading_baseline, learning_speed_baseline, content_baseline, lookup_unit_multiplier, lookup_speed_multiplier, current_step_extra, cluster_normalize_multiplier, cluster_normalize_shift]).astype(jnp.bfloat16)


def steps_of(own_key, dims, cuts, smallest, largest):
    level = 1.0
    for dim, blocks in cuts:
        steps = jax.random.uniform(jax.random.fold_in(jax.random.fold_in(own_key, 6), dim), (blocks,), jnp.float32, smallest / len(cuts), largest / len(cuts))
        level = level * jnp.repeat(jnp.exp(steps), dims[dim] // blocks).reshape((-1,) + (1,) * (len(dims) - 1 - dim))
    return level


def bell_draw(stream_key, dims, scale, bound, shards=(), kind=jnp.bfloat16):
    entries = scale * jax.random.normal(stream_key, dims, jnp.float32)
    if shards:
        entries = entries * steps_of(stream_key, dims, shards, -0.22, 0.18)
    return jnp.clip(entries, -bound, bound).astype(kind)


def setup_inputs(seed: int = 0) -> dict:
    seeds = jax.random.split(jax.random.key(seed), 15)
    layer_entry_input = bell_draw(seeds[0], (TOKENS, MODEL_WIDTH), 1.0, 6.0, ((0, 16),))
    first_layer_values = bell_draw(seeds[1], (TOKENS, MODEL_WIDTH), 1.0, 6.0, ((0, 16), (1, 2)))
    segments = draw_segments(jax.random.fold_in(seeds[14], 71), 0)
    cotangent = bell_draw(seeds[3], (TOKENS, MODEL_WIDTH), 1.0, 6.0, ((0, 16),))
    layernorm_gain = jnp.clip(1.0 + 0.1 * jax.random.normal(seeds[4], (2, MODEL_WIDTH), jnp.float32), 0.5, 1.5).astype(jnp.bfloat16)
    layernorm_bias = bell_draw(seeds[5], (2, MODEL_WIDTH), 0.3, 1.75, ((1, 4),))
    token_shift_coefs = jnp.clip(1.0 * jax.random.uniform(seeds[6], (7, MODEL_WIDTH), jnp.float32) ** steps_of(seeds[6], (7, MODEL_WIDTH), ((1, 4),), -0.2, 0.2), 0.0, 1.0).astype(jnp.bfloat16)
    channel_coefficients = draw_channel_coefficients(jax.random.fold_in(seeds[14], 71), 0)
    receptance_key_value_weight = bell_draw(seeds[8], (3, MODEL_WIDTH, MODEL_WIDTH), MODEL_WIDTH ** -0.5, 0.1875, ((1, 4), (2, 2)))
    output_weight = bell_draw(seeds[9], (MODEL_WIDTH, MODEL_WIDTH), (MODEL_WIDTH // 4) ** -0.5, 0.375, ((0, 2), (1, 4)))
    low_rank_down = bell_draw(seeds[10], (MODEL_WIDTH, LOW_RANK_TOTAL), MODEL_WIDTH ** -0.5, 0.1875, ((0, 4),))
    low_rank_upper = bell_draw(seeds[11], (LOW_RANK_TOTAL, MODEL_WIDTH), DECAY_LOW_RANK ** -0.5, 0.75, ((0, 4), (1, 2)))
    channel_key_weight = bell_draw(seeds[12], (MODEL_WIDTH, FF), MODEL_WIDTH ** -0.5, 0.1875, ((0, 4), (1, 2)))
    channel_value_weight = bell_draw(seeds[13], (FF, MODEL_WIDTH), FF ** -0.5, 0.09375, ((0, 2), (1, 4)))
    return {"layer_entry_input": layer_entry_input, "first_layer_values": first_layer_values, "segments": segments, "cotangent": cotangent, "layernorm_gain": layernorm_gain, "layernorm_bias": layernorm_bias, "token_shift_coefs": token_shift_coefs, "channel_coefficients": channel_coefficients, "receptance_key_value_weight": receptance_key_value_weight, "output_weight": output_weight, "low_rank_down": low_rank_down, "low_rank_upper": low_rank_upper, "channel_key_weight": channel_key_weight, "channel_value_weight": channel_value_weight}


@jax.custom_vjp
def low_rank_hidden(v):
    return lax.optimization_barrier(v.astype(jnp.bfloat16)).astype(jnp.float32)

@jax.custom_vjp
def low_rank_backward(v):
    return v

def low_keep(v):
    return (low_rank_hidden(v), None)

def low_pass(kept, grad):
    return (grad,)

def back_keep(v):
    return (v, None)

def back_low(kept, grad):
    return (low_rank_hidden(grad),)
low_rank_hidden.defvjp(low_keep, low_pass)
low_rank_backward.defvjp(back_keep, back_low)
highest = lax.Precision.HIGHEST
steps_per_block = 16

def matrix_product(left, right):
    return jnp.dot(left, right, precision=highest)

def layer_norm(values, gain, bias):
    mean = lax.optimization_barrier(jnp.mean(values, -1, keepdims=True))
    centred = values - mean
    spread = lax.optimization_barrier(jnp.mean(centred * centred, -1, keepdims=True))
    return centred * lax.rsqrt(spread + 1e-05) * gain + bias

def token_mix(standardized_vectors, keep, blend_amounts):
    shifted = jnp.concatenate([jnp.zeros_like(standardized_vectors[:, :1]), standardized_vectors[:, :-1]], 1) * keep[..., None]
    delta = shifted - standardized_vectors
    return [standardized_vectors + delta * blend_amounts[index_value] for index_value in range(blend_amounts.shape[0])]

def head_leading(receptance_before, key_before_norm, value_before_mix, decay_low_rank, rate_low_rank, value_low_rank, first_layer_values, blend_amounts):

    def split_parts(item_entry):
        return item_entry.reshape(item_entry.shape[:-1] + (H, HS))
    decay_logarithm = -jax.nn.softplus(-(blend_amounts[0] + split_parts(decay_low_rank))) - 0.5
    decay_factor = jnp.exp(-jnp.exp(decay_logarithm))
    rate_values = jax.nn.sigmoid(blend_amounts[1] + split_parts(rate_low_rank))
    lookup_projected_vectors = split_parts(key_before_norm)
    content_projected_vectors = split_parts(value_before_mix)
    content_projected_vectors = content_projected_vectors + (split_parts(first_layer_values) - content_projected_vectors) * jax.nn.sigmoid(blend_amounts[2] + split_parts(value_low_rank))
    removal = lookup_projected_vectors * blend_amounts[3]
    removal = removal * lax.rsqrt(lax.optimization_barrier(jnp.sum(removal * removal, -1, keepdims=True)) + 1e-06)
    lookup_projected_vectors = lookup_projected_vectors * (1.0 + (rate_values - 1.0) * blend_amounts[4])
    return (split_parts(receptance_before), decay_factor, lookup_projected_vectors, content_projected_vectors, -removal, removal * rate_values)

def chain(acceptance_vectors, decay_factor, lookup_projected_vectors, content_projected_vectors, removal_direction, insert_direction, keep):
    batch, length, heads, width = acceptance_vectors.shape
    blocks = length // steps_per_block

    def one_block(state, inputs):
        r_blk, d_blk, k_blk, v_blk, a_blk, b_blk, m_blk = inputs
        outputs = []
        for position in range(steps_per_block):
            state = state * m_blk[position][:, None, None, None]
            pulled = jnp.einsum('bhvk,bhk->bhv', state, a_blk[position], precision=highest)
            state = state * d_blk[position][:, :, None, :] + pulled[..., None] * b_blk[position][:, :, None, :] + v_blk[position][..., None] * k_blk[position][:, :, None, :]
            outputs.append(jnp.einsum('bhvk,bhk->bhv', state, r_blk[position], precision=highest))
        return (state, jnp.stack(outputs))

    def arrange(item_entry):
        item_entry = jnp.moveaxis(item_entry, 1, 0)
        return item_entry.reshape((blocks, steps_per_block) + item_entry.shape[1:])
    inputs = tuple((arrange(item_entry) for item_entry in (acceptance_vectors, decay_factor, lookup_projected_vectors, content_projected_vectors, removal_direction, insert_direction, keep)))
    start = jnp.zeros((batch, heads, width, width), jnp.float32)
    _, outputs = lax.scan(jax.checkpoint(one_block), start, inputs)
    outputs = outputs.reshape((length,) + outputs.shape[2:])
    return jnp.moveaxis(outputs, 0, 1)

def head_trailing(raw_output, acceptance_vectors, lookup_projected_vectors, content_projected_vectors, gate, blend_amounts):
    mean = lax.optimization_barrier(jnp.mean(raw_output, -1, keepdims=True))
    centred = raw_output - mean
    spread = lax.optimization_barrier(jnp.mean(centred * centred, -1, keepdims=True))
    standardized_vectors = centred * lax.rsqrt(spread + 0.00064) * blend_amounts[6] + blend_amounts[7]
    current_step_extra = lax.optimization_barrier(jnp.sum(acceptance_vectors * lookup_projected_vectors * blend_amounts[5], -1, keepdims=True)) * content_projected_vectors
    combined_result = standardized_vectors + current_step_extra
    return combined_result.reshape(gate.shape) * gate

def layer(inputs, first_entry, keep, gains, biases, mixes, blend_amounts, proj, out_proj, down, upper_factor, ffn_in, ffn_out):
    boundary_first = DECAY_LOW_RANK
    boundary_second = boundary_first + RATE_RANK
    boundary_third = boundary_second + VALUE_RANK
    standardized_vectors = layer_norm(inputs, gains[0], biases[0])
    mixed = [low_rank_hidden(item_entry) for item_entry in token_mix(standardized_vectors, keep, mixes[:6])]
    receptance_before = low_rank_backward(matrix_product(mixed[0], proj[0]))
    key_before_norm = low_rank_backward(matrix_product(mixed[2], proj[1]))
    value_before_mix = low_rank_backward(matrix_product(mixed[3], proj[2]))
    decay_inner_rows = low_rank_hidden(jnp.tanh(low_rank_backward(matrix_product(mixed[1], down[:, :boundary_first]))))
    rate_inner_rows = low_rank_hidden(low_rank_backward(matrix_product(mixed[4], down[:, boundary_first:boundary_second])))
    value_inner_rows = low_rank_hidden(low_rank_backward(matrix_product(mixed[3], down[:, boundary_second:boundary_third])))
    gate_inner_rows = low_rank_hidden(jax.nn.sigmoid(low_rank_backward(matrix_product(mixed[5], down[:, boundary_third:]))))
    decay_low_rank = low_rank_backward(matrix_product(decay_inner_rows, upper_factor[:boundary_first]))
    rate_low_rank = low_rank_backward(matrix_product(rate_inner_rows, upper_factor[boundary_first:boundary_second]))
    value_low_rank = low_rank_backward(matrix_product(value_inner_rows, upper_factor[boundary_second:boundary_third]))
    gate_low_rank = low_rank_backward(matrix_product(gate_inner_rows, upper_factor[boundary_third:]))
    acceptance_vectors, decay_factor, lookup_projected_vectors, content_projected_vectors, removal_direction, insert_direction = head_leading(receptance_before, key_before_norm, value_before_mix, decay_low_rank, rate_low_rank, value_low_rank, first_entry, blend_amounts)
    raw_output = chain(acceptance_vectors, decay_factor, lookup_projected_vectors, content_projected_vectors, removal_direction, insert_direction, keep)
    combined_result = low_rank_hidden(head_trailing(raw_output, acceptance_vectors, lookup_projected_vectors, content_projected_vectors, gate_low_rank, blend_amounts))
    mid = inputs + low_rank_backward(matrix_product(combined_result, out_proj))
    normed2 = layer_norm(mid, gains[1], biases[1])
    mixed2 = low_rank_hidden(token_mix(normed2, keep, mixes[6:])[0])
    pre2 = low_rank_backward(matrix_product(mixed2, ffn_in))
    active = jax.nn.relu(pre2)
    hidden2 = low_rank_hidden(active * active)
    return mid + low_rank_backward(matrix_product(hidden2, ffn_out))

def reference(layer_entry_input, first_layer_values, segments, cotangent, layernorm_gain, layernorm_bias, token_shift_coefs, channel_coefficients, receptance_key_value_weight, output_weight, low_rank_down, low_rank_upper, channel_key_weight, channel_value_weight):
    group = math.gcd(SEQS, 4)
    count = SEQS // group
    ids = segments.reshape(SEQS, SEQ_LEN)
    keep = jnp.concatenate([jnp.zeros((SEQS, 1), jnp.float32), (ids[:, 1:] == ids[:, :-1]).astype(jnp.float32)], 1)
    keep = keep.reshape(count, group, SEQ_LEN)
    parameter_set = tuple((item_entry.astype(jnp.float32) for item_entry in (layernorm_gain, layernorm_bias, token_shift_coefs, channel_coefficients, receptance_key_value_weight, output_weight, low_rank_down, low_rank_upper, channel_key_weight, channel_value_weight)))

    def forward(inputs, firsts, *weights):

        def run(pieces):
            return layer(pieces[0], pieces[1], pieces[2], *weights)
        outputs = lax.map(jax.checkpoint(run), (inputs.reshape(count, group, SEQ_LEN, MODEL_WIDTH), firsts.reshape(count, group, SEQ_LEN, MODEL_WIDTH), keep))
        return outputs.reshape(TOKENS, MODEL_WIDTH)
    result, pullback = jax.vjp(forward, layer_entry_input.astype(jnp.float32), first_layer_values.astype(jnp.float32), *parameter_set)
    grads = pullback(cotangent.astype(jnp.float32))
    mix_rows = jnp.concatenate([grads[4][:1], grads[4][2:]], 0)
    return (result.astype(jnp.bfloat16), grads[0], grads[1], grads[2], grads[3], mix_rows, grads[4][1], grads[5], grads[6], grads[7], grads[8], grads[9], grads[10], grads[11])
```

```python
import functools
import math

import jax
import jax.numpy as jnp
from jax import lax
from jax.experimental import pallas as pl
from jax.experimental.pallas import tpu as pltpu
from jax.sharding import PartitionSpec as P

DECAY_LOW_RANK = 64
RATE_RANK = 64
VALUE_RANK = 32


highest = lax.Precision.HIGHEST


def passed_along(block, axis, distance):
    devices = range(lax.axis_size(axis))
    route = [(i - distance, i) for i in devices if i - distance in devices]
    return lax.ppermute(block, axis, route)


def matrix_product(left, right):
    return jnp.dot(left, right, preferred_element_type=jnp.float32)


def inner_product(left, right):
    return lax.dot_general(
        left, right, (((0,), (0,)), ((), ())), preferred_element_type=jnp.float32
    )


def across_heads(left, right):
    return lax.dot_general(
        left, right, (((1,), (1,)), ((), ())), preferred_element_type=jnp.float32
    )


def layer_norm(values, gain, bias):
    mean = jnp.mean(values, -1, keepdims=True)
    centred = values - mean
    spread = jnp.mean(centred * centred, -1, keepdims=True)
    return centred * lax.rsqrt(spread + 1e-05) * gain + bias


def token_mix(standardized_vectors, prev_row, keep, blend_amounts):
    shifted = jnp.concatenate([prev_row, standardized_vectors[:-1]], 0) * keep[:, None]
    delta = shifted - standardized_vectors
    return standardized_vectors[None] + delta[None] * blend_amounts[:, None, :]


def head_leading(
    receptance_before,
    key_before_norm,
    value_before_mix,
    decay_low_rank,
    rate_low_rank,
    value_low_rank,
    first_layer_values,
    blend_amounts,
):
    count = receptance_before.shape[0]
    heads = blend_amounts.shape[1]

    def split_parts(item_entry):
        return item_entry.reshape(count, heads, -1)

    decay_logarithm = -jax.nn.softplus(-(blend_amounts[0] + split_parts(decay_low_rank))) - 0.5
    log_decay = -jnp.exp(decay_logarithm)
    rate_values = jax.nn.sigmoid(blend_amounts[1] + split_parts(rate_low_rank))
    lookup_projected_vectors = split_parts(key_before_norm)
    content_projected_vectors = split_parts(value_before_mix)
    content_projected_vectors = content_projected_vectors + (
        split_parts(first_layer_values) - content_projected_vectors
    ) * jax.nn.sigmoid(blend_amounts[2] + split_parts(value_low_rank))
    removal = lookup_projected_vectors * blend_amounts[3]
    removal = removal * lax.rsqrt(jnp.sum(removal * removal, -1, keepdims=True) + 1e-06)
    lookup_projected_vectors = lookup_projected_vectors * (
        1.0 + (rate_values - 1.0) * blend_amounts[4]
    )
    return (
        split_parts(receptance_before),
        log_decay,
        lookup_projected_vectors,
        content_projected_vectors,
        -removal,
        removal * rate_values,
    )


def exact_dot(left, right, left_dim, right_dim):
    return lax.dot_general(
        left,
        right,
        (((left_dim,), (right_dim,)), ((), ())),
        precision=highest,
        preferred_element_type=jnp.float32,
    )


def block_masks(reset_column, reset_row):
    length = reset_column.shape[0]
    rows = lax.broadcasted_iota(jnp.int32, (length, length), 0)
    cols = lax.broadcasted_iota(jnp.int32, (length, length), 1)
    same = reset_column == reset_row
    return rows, cols, (cols < rows) & same, (cols <= rows) & same


def scaled_parts(r, k, a, b, total, log_w, first, same_last):
    length = total.shape[0]
    before = total - log_w
    centre = total[length // 2 - 1 : length // 2]
    last = total[length - 1 : length]
    grow_before = jnp.exp(before - centre)
    grow_total = jnp.exp(total - centre)
    shrink = jnp.exp(centre - total)
    start_before = jnp.exp(before) * first
    start_total = jnp.exp(total) * first
    tail = jnp.exp(last - total) * same_last
    return grow_before, grow_total, shrink, start_before, start_total, tail, jnp.exp(last)


def chain_forward_kernel(
    r_ref, w_ref, k_ref, v_ref, a_ref, b_ref, col_ref, row_ref,
    raw_trans_ref, raw_off_ref, state_ref, inverse_ref, pull_state_ref, pull_own_ref,
):
    width = state_ref.shape[1]
    heads = state_ref.shape[0]
    length = r_ref.shape[0]
    col = col_ref[...]
    rows, cols, mask_before, mask_after = block_masks(col, row_ref[...])
    first = (col == 0.0).astype(jnp.float32)
    same_last = (col == col[length - 1 : length]).astype(jnp.float32)
    log_all = w_ref[...]
    total_all = exact_dot((cols <= rows).astype(jnp.float32), log_all, 1, 0)
    unit = (cols == rows).astype(jnp.float32)
    here = [slice(h * width, (h + 1) * width) for h in range(heads)]
    stage = []
    for h in range(heads):
        at = here[h]
        r, k, a, b, v = r_ref[:, at], k_ref[:, at], a_ref[:, at], b_ref[:, at], v_ref[:, at]
        gb, gt, sh, sb, st, tail, end = scaled_parts(
            r, k, a, b, total_all[:, at], log_all[:, at], first, same_last
        )
        left = jnp.concatenate([a * gb, r * gt], 0)
        right = jnp.concatenate([b * sh, k * sh], 0)
        cross = exact_dot(left, right, 1, 1)
        l_pull = jnp.where(mask_before, cross[:length, :length], 0.0)
        l_key = jnp.where(mask_before, cross[:length, length:], 0.0)
        q_pull = jnp.where(mask_after, cross[length:, :length], 0.0)
        q_key = jnp.where(mask_after, cross[length:, length:], 0.0)
        stage.append((l_pull, l_key, q_pull, q_key, a * sb, r * st, b * tail, k * tail, v, end))
    solvers = [
        unit + jnp.where(rows // 2 == cols // 2, stage[h][0], 0.0) for h in range(heads)
    ]
    size = 2
    while size < length:
        strip = (rows // (2 * size) == cols // (2 * size)) & (rows // size != cols // size)
        inner = [
            exact_dot(jnp.where(strip, stage[h][0], 0.0), solvers[h], 1, 0) for h in range(heads)
        ]
        solvers = [solvers[h] + exact_dot(solvers[h], inner[h], 1, 0) for h in range(heads)]
        size *= 2
    for h in range(heads):
        at = here[h]
        l_pull, l_key, q_pull, q_key, a0, r0, b_tail, k_tail, v, end = stage[h]
        keyed = exact_dot(l_key, v, 1, 0)
        both = exact_dot(solvers[h], jnp.concatenate([a0, keyed], 1), 1, 0)
        pull_state, pull_own = both[:, :width], both[:, width:]
        out = exact_dot(q_pull, both, 1, 0)
        raw_trans_ref[:, at] = r0 + out[:, :width]
        raw_off_ref[:, at] = out[:, width:] + exact_dot(q_key, v, 1, 0)
        final = exact_dot(both, b_tail, 0, 0)
        diagonal = jnp.where(
            lax.broadcasted_iota(jnp.int32, (width, width), 0)
            == lax.broadcasted_iota(jnp.int32, (width, width), 1),
            end * first[length - 1 : length],
            0.0,
        )
        state_ref[h, :, :width] = final[:width] + diagonal
        state_ref[h, :, width:] = final[width:] + exact_dot(v, k_tail, 0, 0)
        inverse_ref[h] = solvers[h]
        pull_state_ref[:, at] = pull_state
        pull_own_ref[:, at] = pull_own


def chain_backward_kernel(
    r_ref, w_ref, k_ref, v_ref, a_ref, b_ref, col_ref, row_ref,
    inverse_ref, pull_state_ref, pull_own_ref, start_ref, d_end_ref, d_raw_ref,
    dr_ref, dw_ref, dk_ref, dv_ref, da_ref, db_ref,
):
    width = start_ref.shape[1]
    heads = start_ref.shape[0]
    length = r_ref.shape[0]
    col = col_ref[...]
    rows, cols, mask_before, mask_after = block_masks(col, row_ref[...])
    first = (col == 0.0).astype(jnp.float32)
    same_last = (col == col[length - 1 : length]).astype(jnp.float32)
    log_all = w_ref[...]
    total_all = exact_dot((cols <= rows).astype(jnp.float32), log_all, 1, 0)
    is_last = lax.broadcasted_iota(jnp.int32, (length, width), 0) == length - 1
    reverse = (cols >= rows).astype(jnp.float32)
    for h in range(heads):
        at = slice(h * width, (h + 1) * width)
        r, k, a, b, v = r_ref[:, at], k_ref[:, at], a_ref[:, at], b_ref[:, at], v_ref[:, at]
        start, d_end, d_raw = start_ref[h], d_end_ref[h], d_raw_ref[:, at]
        gb, gt, sh, sb, st, tail, end = scaled_parts(
            r, k, a, b, total_all[:, at], log_all[:, at], first, same_last
        )
        a_s, r_s, b_s, k_s = a * gb, r * gt, b * sh, k * sh
        a0, r0, b_tail, k_tail = a * sb, r * st, b * tail, k * tail
        left = jnp.concatenate([a_s, r_s], 0)
        right = jnp.concatenate([b_s, k_s], 0)
        cross = exact_dot(left, right, 1, 1)
        l_key = jnp.where(mask_before, cross[:length, length:], 0.0)
        q_pull = jnp.where(mask_after, cross[length:, :length], 0.0)
        q_key = jnp.where(mask_after, cross[length:, length:], 0.0)
        pulled = pull_own_ref[:, at] + exact_dot(pull_state_ref[:, at], start, 1, 1)
        d_pulled = exact_dot(q_pull, d_raw, 0, 0) + exact_dot(b_tail, d_end, 1, 1)
        d_right = exact_dot(inverse_ref[h], d_pulled, 0, 0)
        dv_ref[:, at] = (
            exact_dot(q_key, d_raw, 0, 0)
            + exact_dot(k_tail, d_end, 1, 1)
            + exact_dot(l_key, d_right, 0, 0)
        )
        d_left_rows = jnp.concatenate([d_right, d_raw], 0)
        d_cross = exact_dot(d_left_rows, jnp.concatenate([pulled, v], 0), 1, 1)
        mask_left = jnp.concatenate([mask_before, mask_after], 0)
        d_cross = jnp.where(jnp.concatenate([mask_left, mask_left], 1), d_cross, 0.0)
        d_left = exact_dot(d_cross, right, 1, 0)
        d_scaled = exact_dot(d_cross, left, 0, 0)
        d_a_s, d_r_s = d_left[:length], d_left[length:]
        d_b_s, d_k_s = d_scaled[:length], d_scaled[length:]
        d_start = exact_dot(d_left_rows, start, 1, 0)
        d_a0, d_r0 = d_start[:length], d_start[length:]
        d_tail = exact_dot(jnp.concatenate([pulled, v], 0), d_end, 1, 0)
        d_b_tail, d_k_tail = d_tail[:length], d_tail[length:]
        da_ref[:, at] = d_a_s * gb + d_a0 * sb
        dr_ref[:, at] = d_r_s * gt + d_r0 * st
        db_ref[:, at] = d_b_s * sh + d_b_tail * tail
        dk_ref[:, at] = d_k_s * sh + d_k_tail * tail
        tails = d_b_tail * b_tail + d_k_tail * k_tail
        d_before = d_a_s * a_s + d_a0 * a0
        d_total = d_before + d_r_s * r_s + d_r0 * r0 - d_b_s * b_s - d_k_s * k_s - tails
        d_last = (
            jnp.sum(tails, 0, keepdims=True)
            + jnp.sum(start * d_end, 0, keepdims=True) * end * first[length - 1 : length]
        )
        d_total = d_total + jnp.where(is_last, d_last, 0.0)
        dw_ref[:, at] = exact_dot(reverse, d_total, 1, 0) - d_before


def chain_specs(length, heads, width, group):
    wide = pl.BlockSpec((length, group * width), lambda i: (0, i))
    col = pl.BlockSpec((length, 1), lambda i: (0, 0))
    row = pl.BlockSpec((1, length), lambda i: (0, 0))
    square = pl.BlockSpec((group, length, length), lambda i: (i, 0, 0))
    state = pl.BlockSpec((group, width, width), lambda i: (i, 0, 0))
    state2 = pl.BlockSpec((group, width, 2 * width), lambda i: (i, 0, 0))
    return wide, col, row, square, state, state2


def run_chain(rows, resets, heads, width):
    length = resets.shape[0]
    group = math.gcd(heads, 4)
    wide, col, row, square, state, state2 = chain_specs(length, heads, width, group)
    f32 = jnp.float32
    flat = jax.ShapeDtypeStruct((length, heads * width), f32)
    return pl.pallas_call(
        chain_forward_kernel,
        grid=(heads // group,),
        in_specs=[wide] * 6 + [col, row],
        out_specs=[wide, wide, state2, square, wide, wide],
        out_shape=[
            flat,
            flat,
            jax.ShapeDtypeStruct((heads, width, 2 * width), f32),
            jax.ShapeDtypeStruct((heads, length, length), f32),
            flat,
            flat,
        ],
        compiler_params=pltpu.CompilerParams(vmem_limit_bytes=40 * 1024 * 1024),
        cost_estimate=pl.CostEstimate(
            flops=heads * 20 * 2 * length**3 * 6, bytes_accessed=4 * 1024 * 1024, transcendentals=0
        ),
    )(*rows, resets[:, None], resets[None, :])


def run_chain_back(rows, resets, saved, start, d_end, d_raw):
    length = resets.shape[0]
    heads, width = start.shape[0], start.shape[1]
    group = math.gcd(heads, 4)
    wide, col, row, square, state, state2 = chain_specs(length, heads, width, group)
    flat = jax.ShapeDtypeStruct((length, heads * width), jnp.float32)
    return pl.pallas_call(
        chain_backward_kernel,
        grid=(heads // group,),
        in_specs=[wide] * 6 + [col, row, square, wide, wide, state, state, wide],
        out_specs=[wide] * 6,
        out_shape=[flat] * 6,
        compiler_params=pltpu.CompilerParams(vmem_limit_bytes=40 * 1024 * 1024),
        cost_estimate=pl.CostEstimate(
            flops=heads * 20 * 2 * length**3 * 6, bytes_accessed=6 * 1024 * 1024, transcendentals=0
        ),
    )(*rows, resets[:, None], resets[None, :], *saved, start, d_end, d_raw)


def state_before(gathered):
    place = lax.axis_index("ctx")
    width = gathered.shape[2]
    state = jnp.zeros(gathered.shape[1:3] + (width,), jnp.float32)
    for hop in range(gathered.shape[0] - 1):
        part = gathered[hop]
        new = (
            jnp.einsum("hij,hjk->hik", state, part[..., :width], precision=highest)
            + part[..., width:]
        )
        state = jnp.where(hop < place, new, state)
    return state


def state_gradient_after(gathered, local):
    place = lax.axis_index("ctx")
    width = gathered.shape[2]
    state = jnp.zeros(gathered.shape[1:3] + (width,), jnp.float32)
    for hop in range(gathered.shape[0] - 1, 0, -1):
        new = (
            jnp.einsum("hij,hkj->hik", state, gathered[hop][..., :width], precision=highest)
            + local[hop].astype(jnp.float32)
        )
        state = jnp.where(hop > place, new, state)
    return state


def head_trailing(
    raw_output,
    acceptance_vectors,
    lookup_projected_vectors,
    content_projected_vectors,
    gate,
    blend_amounts,
):
    mean = jnp.mean(raw_output, -1, keepdims=True)
    centred = raw_output - mean
    spread = jnp.mean(centred * centred, -1, keepdims=True)
    standardized_vectors = (
        centred * lax.rsqrt(spread + 0.00064) * blend_amounts[6] + blend_amounts[7]
    )
    current_step_extra = (
        jnp.sum(acceptance_vectors * lookup_projected_vectors * blend_amounts[5], -1, keepdims=True)
        * content_projected_vectors
    )
    combined_result = standardized_vectors + current_step_extra
    return combined_result.reshape(gate.shape) * gate


def row_tile(height, width):
    for tile in (256, 128, 64, 32):
        if height % tile == 0 and tile * width <= 32768:
            return tile
    return 16


def reduce_kernel(count, owners, blocks, *refs):
    parts, outs = refs[:count], refs[count : 2 * count]
    landed, mine, arrived = (refs[(2 + k) * count : (3 + k) * count] for k in range(3))
    own_sem, s1, r1, s2, r2, s3, r3 = refs[5 * count :]
    place, owner = lax.axis_index("ctx"), lax.axis_index("shard")
    mesh_id = pl.DeviceIdType.MESH

    def peer(index, step, size):
        return lax.rem(index + step, size)

    barrier = pltpu.get_barrier_semaphore()
    for d in range(1, blocks):
        pl.semaphore_signal(
            barrier, inc=1, device_id={"ctx": peer(place, d, blocks)}, device_id_type=mesh_id
        )
    for d in range(1, owners):
        pl.semaphore_signal(
            barrier, inc=1, device_id={"shard": peer(owner, d, owners)}, device_id_type=mesh_id
        )
    pl.semaphore_wait(barrier, blocks + owners - 2)

    first, second, third, local = {}, {}, {}, []
    for p in range(count):
        local.append(pltpu.make_async_copy(parts[p].at[:, place], mine[p], own_sem.at[p]))
        local[p].start()
        for d in range(1, blocks):
            to = peer(place, d, blocks)
            first[p, d] = pltpu.make_async_remote_copy(
                src_ref=parts[p].at[:, to],
                dst_ref=landed[p].at[d - 1],
                send_sem=s1.at[p, d - 1],
                recv_sem=r1.at[p, d - 1],
                device_id={"ctx": to},
                device_id_type=mesh_id,
            )
            first[p, d].start()

    def finish(p):
        for d in range(1, owners):
            second[p, d].wait_recv()
        height, width = mine[p].shape[1:]
        tile = row_tile(height, width)

        @pl.loop(0, height // tile)
        def _(t):
            at = pl.ds(pl.multiple_of(t * tile, tile), tile)
            total = mine[p][owner, at, :].astype(jnp.float32)
            for d in range(owners - 1):
                total = total + arrived[p][d, at, :].astype(jnp.float32)
            outs[p][place, at, :] = total.astype(jnp.bfloat16)

        for d in range(1, blocks):
            third[p, d] = pltpu.make_async_remote_copy(
                src_ref=outs[p].at[place],
                dst_ref=outs[p].at[place],
                send_sem=s3.at[p, d - 1],
                recv_sem=r3.at[p, d - 1],
                device_id={"ctx": peer(place, d, blocks)},
                device_id_type=mesh_id,
            )
            third[p, d].start()

    for p in range(count):
        local[p].wait()
        for d in range(1, blocks):
            first[p, d].wait_recv()
        height, width = mine[p].shape[1:]
        tile = row_tile(height, width)
        steps = height // tile

        @pl.loop(0, owners)
        def _(s):
            @pl.loop(0, steps)
            def _(t):
                at = pl.ds(pl.multiple_of(t * tile, tile), tile)
                total = mine[p][s, at, :].astype(jnp.float32)
                for d in range(blocks - 1):
                    total = total + landed[p][d, s, at, :].astype(jnp.float32)
                mine[p][s, at, :] = total.astype(jnp.bfloat16)

        for d in range(1, owners):
            to = peer(owner, d, owners)
            second[p, d] = pltpu.make_async_remote_copy(
                src_ref=mine[p].at[to],
                dst_ref=arrived[p].at[d - 1],
                send_sem=s2.at[p, d - 1],
                recv_sem=r2.at[p, d - 1],
                device_id={"shard": to},
                device_id_type=mesh_id,
            )
            second[p, d].start()
        if p > 0:
            finish(p - 1)
    finish(count - 1)
    for p in range(count):
        for d in range(1, blocks):
            third[p, d].wait_recv()
    for copies in (first, second, third):
        for copy in copies.values():
            copy.wait_send()


def reduce_parts(parts):
    owners, blocks = lax.axis_size("shard"), lax.axis_size("ctx")
    count = len(parts)
    bf16 = jnp.bfloat16
    shapes = [part.shape[2:] for part in parts]
    dma = pltpu.SemaphoreType.DMA
    return pl.pallas_call(
        functools.partial(reduce_kernel, count, owners, blocks),
        in_specs=[pl.BlockSpec(memory_space=pl.ANY)] * count,
        out_specs=[pl.BlockSpec(memory_space=pltpu.VMEM)] * count,
        out_shape=[jax.ShapeDtypeStruct((blocks,) + shape, bf16) for shape in shapes],
        scratch_shapes=[pltpu.VMEM((blocks - 1, owners) + shape, bf16) for shape in shapes]
        + [pltpu.VMEM((owners,) + shape, bf16) for shape in shapes]
        + [pltpu.VMEM((owners - 1,) + shape, bf16) for shape in shapes]
        + [
            dma((count,)),
            dma((count, blocks - 1)),
            dma((count, blocks - 1)),
            dma((count, owners - 1)),
            dma((count, owners - 1)),
            dma((count, blocks - 1)),
            dma((count, blocks - 1)),
        ],
        compiler_params=pltpu.CompilerParams(
            collective_id=3, has_side_effects=True, vmem_limit_bytes=48 * 1024 * 1024
        ),
    )(*parts)


def sum_gradients(members):
    owners, blocks = lax.axis_size("shard"), lax.axis_size("ctx")
    views, flat, loose = [], [], []
    for index, member in enumerate(members):
        _, height, width = member.shape
        member = member.astype(jnp.bfloat16)
        if height % (16 * blocks) == 0 and width % 128 == 0:
            views.append((index, member.reshape(owners, blocks, height // blocks, width)))
        else:
            loose.append(index)
            flat.append(member.reshape(owners, -1))
    sizes = [part.shape[1] for part in flat]
    joined = jnp.concatenate(flat, 1)
    unit = blocks * 128 * 32
    joined = jnp.pad(joined, ((0, 0), (0, -joined.shape[1] % unit)))
    joined = joined.reshape(owners, blocks, -1, 128)
    summed = reduce_parts([view for _, view in views] + [joined])
    result = {}
    for (index, view), total in zip(views, summed):
        result[index] = total.reshape(members[index].shape[1:]).astype(jnp.float32)
    rest = summed[-1].reshape(-1).astype(jnp.float32)
    begin = 0
    for index, size in zip(loose, sizes):
        result[index] = rest[begin : begin + size].reshape(members[index].shape[1:])
        begin += size
    return [result[index] for index in range(len(members))]


def per_device(
    layer_entry_input,
    first_layer_values,
    segments,
    cotangent,
    layernorm_gain,
    layernorm_bias,
    token_shift_coefs,
    channel_coefficients,
    receptance_key_value_weight,
    output_weight,
    low_rank_down,
    low_rank_upper,
    channel_key_weight,
    channel_value_weight,
):
    gains, biases, mixes, blend_amounts, proj, out_proj, down, upper_factor, ffn_in, ffn_out = (
        lax.all_gather(layernorm_gain, "shard", axis=1, tiled=True),
        lax.all_gather(layernorm_bias, "shard", axis=1, tiled=True),
        lax.all_gather(token_shift_coefs, "shard", axis=1, tiled=True),
        lax.all_gather(channel_coefficients, "shard", axis=2, tiled=True),
        lax.all_gather(receptance_key_value_weight, "shard", axis=1, tiled=True),
        lax.all_gather(output_weight, "shard", axis=1, tiled=True),
        lax.all_gather(low_rank_down, "shard", axis=0, tiled=True),
        lax.all_gather(low_rank_upper, "shard", axis=0, tiled=True),
        lax.all_gather(channel_key_weight, "shard", axis=0, tiled=True),
        lax.all_gather(channel_value_weight, "shard", axis=1, tiled=True),
    )
    gains = gains.astype(jnp.float32)
    biases = biases.astype(jnp.float32)
    mixes = mixes.astype(jnp.float32)
    blend_amounts = blend_amounts.astype(jnp.float32)
    boundary_first = DECAY_LOW_RANK
    boundary_second = boundary_first + RATE_RANK
    boundary_third = boundary_second + VALUE_RANK
    inputs_f = layer_entry_input.astype(jnp.float32)
    seg_next = (segments + 1).astype(jnp.float32)
    standardized_vectors, norm1_back = jax.vjp(layer_norm, inputs_f, gains[0], biases[0])
    prev_row, prev_seg = passed_along((standardized_vectors[-1:], seg_next[-1:]), "ctx", 1)
    keep = jnp.concatenate(
        [
            (prev_seg == seg_next[:1]).astype(jnp.float32),
            (segments[1:] == segments[:-1]).astype(jnp.float32),
        ]
    )

    def mix_local(normed_in, prev_in, coef_in):
        return token_mix(normed_in, prev_in, keep, coef_in)

    mix_all, mix1_back = jax.vjp(mix_local, standardized_vectors, prev_row, mixes[:6])
    mixed = mix_all.astype(jnp.bfloat16)
    receptance_before = matrix_product(mixed[0], proj[0])
    key_before_norm = matrix_product(mixed[2], proj[1])
    value_before_mix = matrix_product(mixed[3], proj[2])
    decay_inner_rows = jnp.tanh(matrix_product(mixed[1], down[:, :boundary_first]))
    rate_inner_rows = matrix_product(mixed[4], down[:, boundary_first:boundary_second])
    value_inner_rows = matrix_product(mixed[3], down[:, boundary_second:boundary_third])
    gate_inner_rows = jax.nn.sigmoid(matrix_product(mixed[5], down[:, boundary_third:]))
    hidden_bfloat = [
        item_entry.astype(jnp.bfloat16)
        for item_entry in (decay_inner_rows, rate_inner_rows, value_inner_rows, gate_inner_rows)
    ]
    upper_factor_parts = [
        upper_factor[:boundary_first],
        upper_factor[boundary_first:boundary_second],
        upper_factor[boundary_second:boundary_third],
        upper_factor[boundary_third:],
    ]
    low_rank_maps = [
        matrix_product(hidden_bfloat[index_value], upper_factor_parts[index_value])
        for index_value in range(4)
    ]
    fronts, front_back = jax.vjp(
        head_leading,
        receptance_before,
        key_before_norm,
        value_before_mix,
        low_rank_maps[0],
        low_rank_maps[1],
        low_rank_maps[2],
        first_layer_values.astype(jnp.float32),
        blend_amounts,
    )
    acceptance_vectors, _, lookup_projected_vectors, content_projected_vectors, _, _ = fronts
    heads = blend_amounts.shape[1]
    width = blend_amounts.shape[2]
    count = acceptance_vectors.shape[0]
    rows = [item_entry.reshape(count, heads * width) for item_entry in fronts]
    resets = jnp.cumsum(1.0 - keep)
    raw_trans, raw_off, final_both, *saved = run_chain(rows, resets, heads, width)
    final_both, ffn_in, ffn_out = lax.optimization_barrier((final_both, ffn_in, ffn_out))
    finals = lax.all_gather(final_both, "ctx")
    incoming = state_before(finals)
    raw_trans = raw_trans.reshape(count, heads, width)
    raw_output = raw_off.reshape(count, heads, width) + jnp.einsum(
        "hvi,thi->thv", incoming, raw_trans, precision=highest
    )
    combined_result, trailing_backward = jax.vjp(
        head_trailing,
        raw_output,
        acceptance_vectors,
        lookup_projected_vectors,
        content_projected_vectors,
        low_rank_maps[3],
        blend_amounts,
    )
    merged_bf = combined_result.astype(jnp.bfloat16)
    attn = lax.psum(matrix_product(merged_bf, out_proj).astype(jnp.bfloat16), "tp").astype(
        jnp.float32
    )
    mid = inputs_f + attn
    normed2, norm2_back = jax.vjp(layer_norm, mid, gains[1], biases[1])
    prev2 = passed_along(normed2[-1:], "ctx", 1)
    mix2, mix2_back = jax.vjp(mix_local, normed2, prev2, mixes[6:])
    mix2_bf = mix2[0].astype(jnp.bfloat16)
    pre2 = matrix_product(mix2_bf, ffn_in)
    active = jax.nn.relu(pre2)
    hidden2_bf = (active * active).astype(jnp.bfloat16)
    ffn = lax.psum(matrix_product(hidden2_bf, ffn_out).astype(jnp.bfloat16), "tp").astype(
        jnp.float32
    )
    result = (mid + ffn).astype(jnp.bfloat16)
    owners = lax.axis_size("shard")

    def by_owner(left, right):
        split = right.reshape(right.shape[0], owners, -1)
        return jnp.stack([inner_product(left, split[:, s]) for s in range(owners)])

    g_ffn_out = by_owner(hidden2_bf, cotangent)
    d_pre2 = (across_heads(cotangent, ffn_out) * 2.0 * active).astype(jnp.bfloat16)
    g_ffn_in = inner_product(mix2_bf, d_pre2)
    d_mix2 = lax.psum(across_heads(d_pre2, ffn_in).astype(jnp.bfloat16), "tp").astype(jnp.float32)
    d_normed2, d_prev2, d_coef2 = mix2_back(d_mix2[None])
    d_row2 = passed_along(d_prev2, "ctx", -1)
    d_normed2 = d_normed2.at[-1:].add(d_row2)
    d_mid_norm, d_gain2, d_bias2 = norm2_back(d_normed2)
    d_mid = cotangent.astype(jnp.float32) + d_mid_norm
    d_attn_bf = d_mid.astype(jnp.bfloat16)
    g_out = by_owner(merged_bf, d_attn_bf)
    d_merged = across_heads(d_attn_bf, out_proj)
    d_raw, d_recept_post, d_keyed_post, d_valued_post, d_gate, d_coef_post = trailing_backward(
        d_merged
    )
    local_in = jnp.einsum("thv,thi->hvi", d_raw, raw_trans, precision=highest)
    d_outgoing = state_gradient_after(
        finals, lax.all_gather(local_in.astype(jnp.bfloat16), "ctx")
    )
    chain_grads = [
        item_entry.reshape(count, heads, width)
        for item_entry in run_chain_back(
            rows, resets, saved, incoming, d_outgoing, d_raw.reshape(count, heads * width)
        )
    ]
    front_grads = front_back(
        (
            d_recept_post + chain_grads[0],
            chain_grads[1],
            d_keyed_post + chain_grads[2],
            d_valued_post + chain_grads[3],
            chain_grads[4],
            chain_grads[5],
        )
    )
    d_rp_bf = front_grads[0].astype(jnp.bfloat16)
    d_kp_bf = front_grads[1].astype(jnp.bfloat16)
    d_vp_bf = front_grads[2].astype(jnp.bfloat16)
    low_rank_gradients = [
        front_grads[3].astype(jnp.bfloat16),
        front_grads[4].astype(jnp.bfloat16),
        front_grads[5].astype(jnp.bfloat16),
        d_gate.astype(jnp.bfloat16),
    ]
    d_first = front_grads[6]
    g_head = front_grads[7] + d_coef_post
    g_proj = [
        inner_product(mixed[0], d_rp_bf),
        inner_product(mixed[2], d_kp_bf),
        inner_product(mixed[3], d_vp_bf),
    ]
    gate_up_weight = jnp.concatenate(
        [
            inner_product(hidden_bfloat[index_value], low_rank_gradients[index_value])
            for index_value in range(4)
        ],
        0,
    )
    d_hidden_part = jnp.concatenate(
        [
            across_heads(low_rank_gradients[index_value], upper_factor_parts[index_value])
            for index_value in range(4)
        ],
        1,
    )
    d_xr, d_xk, d_xv, d_hidden = (
        lax.psum(across_heads(d_rp_bf, proj[0]).astype(jnp.bfloat16), "tp").astype(jnp.float32),
        lax.psum(across_heads(d_kp_bf, proj[1]).astype(jnp.bfloat16), "tp").astype(jnp.float32),
        lax.psum(across_heads(d_vp_bf, proj[2]).astype(jnp.bfloat16), "tp").astype(jnp.float32),
        lax.psum(d_hidden_part.astype(jnp.bfloat16), "tp").astype(jnp.float32),
    )
    d_pre_decay = (
        d_hidden[:, :boundary_first] * (1.0 - decay_inner_rows * decay_inner_rows)
    ).astype(jnp.bfloat16)
    d_pre_rate = d_hidden[:, boundary_first:boundary_second].astype(jnp.bfloat16)
    d_pre_value = d_hidden[:, boundary_second:boundary_third].astype(jnp.bfloat16)
    d_pre_gate = (d_hidden[:, boundary_third:] * gate_inner_rows * (1.0 - gate_inner_rows)).astype(
        jnp.bfloat16
    )
    g_down = jnp.concatenate(
        [
            inner_product(mixed[1], d_pre_decay),
            inner_product(mixed[4], d_pre_rate),
            inner_product(mixed[3], d_pre_value),
            inner_product(mixed[5], d_pre_gate),
        ],
        1,
    )
    d_mixes = jnp.stack(
        [
            d_xr,
            across_heads(d_pre_decay, down[:, :boundary_first]),
            d_xk,
            d_xv + across_heads(d_pre_value, down[:, boundary_second:boundary_third]),
            across_heads(d_pre_rate, down[:, boundary_first:boundary_second]),
            across_heads(d_pre_gate, down[:, boundary_third:]),
        ]
    )
    d_normed, d_prev, d_coef1 = mix1_back(d_mixes)
    d_row = passed_along(d_prev, "ctx", -1)
    d_normed = d_normed.at[-1:].add(d_row)
    d_input_norm, d_gain1, d_bias1 = norm1_back(d_normed)
    d_input = d_mid + d_input_norm
    row_grads = jnp.concatenate(
        [jnp.stack([d_gain1, d_gain2]), jnp.stack([d_bias1, d_bias2]), d_coef1, d_coef2], 0
    )

    def columns(member):
        split = member.reshape(member.shape[:-1] + (owners, -1))
        return jnp.moveaxis(split, -2, 0).reshape(owners, -1, split.shape[-1])

    def rows_of(member):
        return member.reshape(owners, -1, member.shape[-1])

    row_sums, sum_head, sum_r, sum_k, sum_v, sum_out, sum_down, sum_up, sum_in, sum_ffn_out = (
        sum_gradients(
            [
                columns(row_grads),
                columns(g_head),
                *[rows_of(member) for member in g_proj],
                g_out,
                rows_of(g_down),
                rows_of(gate_up_weight),
                rows_of(g_ffn_in),
                g_ffn_out,
            ]
        )
    )
    mix_rows = jnp.concatenate([row_sums[4:5], row_sums[6:11]], 0)
    return (
        result,
        d_input,
        d_first,
        row_sums[0:2],
        row_sums[2:4],
        mix_rows,
        row_sums[5],
        sum_head.reshape(g_head.shape[:-1] + (-1,)),
        jnp.stack([sum_r, sum_k, sum_v]),
        sum_out,
        sum_down,
        sum_up,
        sum_in,
        sum_ffn_out,
    )


def solution(mesh):
    return jax.shard_map(
        per_device,
        mesh=mesh,
        in_specs=(
            P(("shard", "ctx"), None),
            P(("shard", "ctx"), "tp"),
            P(("shard", "ctx")),
            P(("shard", "ctx"), None),
            P(None, "shard"),
            P(None, "shard"),
            P(None, "shard"),
            P(None, "tp", "shard"),
            P(None, "shard", "tp"),
            P("tp", "shard"),
            P("shard", None),
            P("shard", "tp"),
            P("shard", "tp"),
            P("tp", "shard"),
        ),
        out_specs=(
            P(("shard", "ctx"), None),
            P(("shard", "ctx"), None),
            P(("shard", "ctx"), "tp"),
            P(None, "shard"),
            P(None, "shard"),
            P(None, "shard"),
            P("shard"),
            P(None, "tp", "shard"),
            P(None, "shard", "tp"),
            P("tp", "shard"),
            P("shard", None),
            P("shard", "tp"),
            P("shard", "tp"),
            P("tp", "shard"),
        ),
        check_vma=False,
    )
```
